32 devices in a mesh: cam: 2 (over x), sp: 16 (over z, y, core).
Axes of the slice: x: 2, y: 2, z: 4, core: 2. Of those that a mesh axis runs over, the one named last changes fastest.
Arguments:
- q_self: bfloat16 [2, 512, 2048], P('cam', 'sp'), may hold values from -8 to 8
- keys: bfloat16 [2, 512, 2048], P('cam', 'sp'), may hold values from -4 to 4
- values: bfloat16 [2, 512, 2048], P('cam', 'sp'), may hold values from -4 to 4
- q_cross: bfloat16 [2, 512, 2048], P('cam', 'sp'), may hold values from -8 to 8
- timestep: int32 [1], replicated, may hold values from 0 to 49
- mod_table: float32 [50, 2, 2048], replicated, may hold values from 0.5 to 3
Outputs:
- block_out: bfloat16 [2, 512, 2048], P('cam', 'sp')
The draws below stay inside these ranges and needn't reach their ends.
All inputs are finite; a program needn't handle non-finite values.
Results may differ from the reference program's by a relative error of at most 0.0042.
Values may be sent and summed in bfloat16 or wider, within the bound.
A program may use at most 64 MiB of HBM per device.

```python
import math
import jax
import jax.numpy as jnp
from jax import lax

HEADS = 16
HEAD_DIM = 128
TOK_DEV = 32
STEPS = 50
CAMS = 2
SEQ = 512
HD = 2048
N_SP = 16


def draw_keys(key, part):
    drawn = jnp.clip(jax.random.normal(jax.random.fold_in(key, 11), (CAMS, SEQ, HD), jnp.float32), -4.0, 4.0)
    return drawn.astype(jnp.bfloat16)


def draw_q_self(key, part):
    drawn = jnp.clip(jax.random.normal(jax.random.fold_in(key, 21), (CAMS, SEQ, HD), jnp.float32), -8.0, 8.0)
    return drawn.astype(jnp.bfloat16)


def draw_q_cross(key, part):
    drawn = jnp.clip(jax.random.normal(jax.random.fold_in(key, 31), (CAMS, SEQ, HD), jnp.float32), -8.0, 8.0)
    return drawn.astype(jnp.bfloat16)


def level_of(stream_key, dims, shards, least, top_value):
    factor_of, own = 1.0, jax.random.fold_in(stream_key, 6)
    for position, parts in shards:
        heights = jnp.exp(jax.random.uniform(jax.random.fold_in(own, position), (parts,), jnp.float32, least / len(shards), top_value / len(shards)))
        factor_of = factor_of * jnp.repeat(heights, dims[position] // parts).reshape([-1 if axis == position else 1 for axis in range(len(dims))])
    return factor_of


def noise(key, shape, deviation, bound, split=(), dtype=jnp.bfloat16):
    factor_of = level_of(key, shape, split, -0.22, 0.18) if split else 1.0
    entries = jax.random.normal(key, shape, jnp.float32) * deviation * factor_of
    return jnp.minimum(jnp.maximum(entries, -bound), bound).astype(dtype)


def setup_inputs(seed: int = 0) -> dict:
    arg_keys = jax.random.split(jax.random.key(seed), 7)
    return {
        "q_self": draw_q_self(jax.random.fold_in(arg_keys[6], 71), 0),
        "keys": draw_keys(jax.random.fold_in(arg_keys[6], 71), 0),
        "values": noise(arg_keys[2], (CAMS, SEQ, HD), 1.0, 4.0, ((0, 2), (1, 16))),
        "q_cross": draw_q_cross(jax.random.fold_in(arg_keys[6], 71), 0),
        "timestep": jax.random.randint(arg_keys[4], (1,), 0, STEPS).astype(jnp.int32),
        "mod_table": jnp.clip(jnp.exp(jax.random.uniform(arg_keys[5], (STEPS, 2, HD), jnp.float32, math.log(0.5), math.log(3.0))), 0.5, 3.0),
    }


def self_attention(q_self, keys, values):
    score_scale = 1.0 / math.sqrt(HEAD_DIM)

    def stack_heads(tensor):
        return tensor.reshape(CAMS, SEQ, HEADS, HEAD_DIM).transpose(0, 2, 1, 3).reshape(CAMS * HEADS, SEQ, HEAD_DIM)

    def per_head(operands):
        query_part, key_part, value_part = operands
        scores = jnp.dot(query_part, key_part.T, preferred_element_type=jnp.float32) * score_scale
        row_peak = lax.optimization_barrier(jnp.max(scores, axis=1))
        weights = jnp.exp(scores - row_peak[:, None])
        totals = lax.optimization_barrier(jnp.sum(weights, axis=1))
        numerator = jnp.dot(weights.astype(jnp.bfloat16), value_part, preferred_element_type=jnp.float32)
        return (numerator / totals[:, None]).astype(jnp.bfloat16)
    result = lax.map(per_head, (stack_heads(q_self), stack_heads(keys), stack_heads(values)))
    return result.reshape(CAMS, HEADS, SEQ, HEAD_DIM).transpose(0, 2, 1, 3).reshape(CAMS, SEQ, HD)

def cross_view(q_cross, keys, values):
    score_scale = 1.0 / math.sqrt(HEAD_DIM)
    shape_five = (CAMS, N_SP, TOK_DEV, HEADS, HEAD_DIM)
    cross_queries = q_cross.reshape(shape_five)
    key_bands = keys.reshape(shape_five)
    value_bands = values.reshape(shape_five)
    near_keys = jnp.concatenate([jnp.roll(key_bands, 1, axis=0), jnp.roll(key_bands, -1, axis=0)], axis=2)
    near_values = jnp.concatenate([jnp.roll(value_bands, 1, axis=0), jnp.roll(value_bands, -1, axis=0)], axis=2)

    def per_camera(operands):
        query_part, key_part, value_part = operands
        scores = jnp.einsum('bqhd,bkhd->bhqk', query_part.astype(jnp.float32), key_part.astype(jnp.float32)) * score_scale
        row_peak = lax.optimization_barrier(jnp.max(scores, axis=3))
        weights = jnp.exp(scores - row_peak[..., None])
        totals = lax.optimization_barrier(jnp.sum(weights, axis=3))
        rounded = lax.optimization_barrier(weights.astype(jnp.bfloat16)).astype(jnp.float32)
        numerator = jnp.einsum('bhqk,bkhd->bqhd', rounded, value_part.astype(jnp.float32))
        return numerator / jnp.swapaxes(totals, 1, 2)[..., None]
    result = lax.map(per_camera, (cross_queries, near_keys, near_values))
    return result.reshape(CAMS, SEQ, HD)

def reference(q_self, keys, values, q_cross, timestep, mod_table):
    self_out = self_attention(q_self, keys, values)
    cross_out = cross_view(q_cross, keys, values)
    gate_rows = mod_table[timestep[0]]
    mixed = gate_rows[0] * self_out.astype(jnp.float32) + gate_rows[1] * cross_out
    return mixed.astype(jnp.bfloat16)
```

```python
import functools
import math

import jax
import jax.numpy as jnp
from jax import lax
from jax.experimental import pallas as pl
from jax.experimental.pallas import tpu as pltpu
from jax.sharding import PartitionSpec as P

HEADS = 16
MESH = pl.DeviceIdType.MESH
LOG2E = 1.4426950408889634


def offsets(count):
    return sorted(range(1, count), key=lambda d: (abs(d - count // 2), d))


def softmax_parts(scores, scale):
    peak = jnp.max(scores, axis=-1, keepdims=True)
    weights = jnp.exp2((scores - peak) * (scale * LOG2E))
    return weights.astype(jnp.bfloat16), jnp.sum(weights, axis=-1, keepdims=True)


def dot_t(a, b):
    return lax.dot_general(a, b, (((1,), (1,)), ((), ())), preferred_element_type=jnp.float32)


def kernel(
    n, cams, step_ref, q_ref, k_ref, v_ref, qc_ref, mod_ref, out_ref,
    q_all, k_all, v_all, near_k, near_v, qc, mod, weights, sums, mine, back, cross,
    send_sem, cross_send, back_send, q_sem, k_sem, v_sem, near_sem, back_sem, qc_sem, mod_sem,
):
    rows, dim = q_all.shape[1], q_all.shape[2]
    heads = HEADS
    copies = n // heads
    sides = near_k.shape[0]
    me = lax.axis_index("sp")
    cam = lax.axis_index("cam")
    head = lax.div(me, copies)
    copy = lax.rem(me, copies)
    my_group = lax.div(me, heads)
    my_slot = lax.rem(me, heads)
    scale = 1.0 / math.sqrt(dim)

    def cols(h):
        return pl.ds(pl.multiple_of(h * dim, dim), dim)

    barrier = pltpu.get_barrier_semaphore()
    for d in offsets(n):
        pl.semaphore_signal(
            barrier, inc=1, device_id={"sp": lax.rem(me + d, n)}, device_id_type=MESH
        )
    for side in range(sides):
        other = lax.rem(cam + (1 if side == 0 else cams - 1), cams)
        pl.semaphore_signal(barrier, inc=1, device_id={"cam": other}, device_id_type=MESH)

    load_qc = pltpu.make_async_copy(qc_ref.at[0], qc, qc_sem)
    load_mod = pltpu.make_async_copy(mod_ref, mod, mod_sem)
    load_qc.start()
    load_mod.start()
    pltpu.make_async_copy(k_ref.at[0, :, cols(head)], k_all.at[me], k_sem).start()
    pltpu.make_async_copy(v_ref.at[0, :, cols(head)], v_all.at[me], v_sem).start()
    in_group = my_group == copy

    @pl.when(in_group)
    def _():
        pltpu.make_async_copy(q_ref.at[0, :, cols(head)], q_all.at[my_slot], q_sem).start()

    pl.semaphore_wait(barrier, n - 1 + sides)

    def send(src, dst, sem, peer):
        pltpu.make_async_remote_copy(
            src_ref=src, dst_ref=dst, send_sem=send_sem, recv_sem=sem,
            device_id={"sp": peer}, device_id_type=MESH,
        ).start()

    for d in offsets(n):
        peer = lax.rem(me + d, n)
        send(k_ref.at[0, :, cols(lax.div(peer, copies))], k_all.at[me], k_sem, peer)
        if copies == 1:
            send(q_ref.at[0, :, cols(peer)], q_all.at[me], q_sem, peer)
    if copies > 1:
        for h in range(heads):
            peer = h * copies + my_group

            @pl.when(peer != me)
            def _():
                send(q_ref.at[0, :, cols(h)], q_all.at[my_slot], q_sem, peer)

    for side in range(sides):
        other = lax.rem(cam + (1 if side == 0 else cams - 1), cams)
        for index, (src, dst) in enumerate(((k_ref, near_k), (v_ref, near_v))):
            pltpu.make_async_remote_copy(
                src_ref=src.at[0], dst_ref=dst.at[side],
                send_sem=cross_send.at[side, index], recv_sem=near_sem.at[side, index],
                device_id={"cam": other}, device_id_type=MESH,
            ).start()
    for d in offsets(n):
        peer = lax.rem(me + d, n)
        send(v_ref.at[0, :, cols(lax.div(peer, copies))], v_all.at[me], v_sem, peer)

    load_qc.wait()
    load_mod.wait()
    for side in range(sides):
        for index, dst in enumerate((near_k, near_v)):
            pltpu.make_async_copy(dst.at[side], dst.at[side], near_sem.at[side, index]).wait()
    gates = mod[step_ref[0]]
    for h in range(heads):
        part = slice(h * dim, (h + 1) * dim)
        keys = near_k[:, :, part].reshape(sides * rows, dim)
        vals = near_v[:, :, part].reshape(sides * rows, dim)
        w, total = softmax_parts(dot_t(qc[:, part], keys), scale)
        result = jnp.dot(w, vals, preferred_element_type=jnp.float32) / total
        cross[:, part] = gates[1:2, part] * result

    pltpu.make_async_copy(k_all, k_all, k_sem).wait()
    pltpu.make_async_copy(q_all, q_all, q_sem).wait()
    per = 4
    blocks = heads // per
    first = lax.div(my_slot, per)
    order = [blocks // 2] + [b for b in range(1, blocks) if b != blocks // 2] + [0]
    keys = k_all[...].reshape(n * rows, dim)
    for index, b in enumerate(order):
        block = lax.rem(first + b, blocks)
        queries = q_all[pl.ds(block * per, per)].reshape(per * rows, dim)
        w, total = softmax_parts(dot_t(queries, keys), scale)
        weights[index] = w
        sums[index] = total
    pltpu.make_async_copy(v_all, v_all, v_sem).wait()
    vals = v_all[...].reshape(n * rows, dim)
    for index, b in enumerate(order):
        block = lax.rem(first + b, blocks)
        result = jnp.dot(weights[index], vals, preferred_element_type=jnp.float32) / sums[index]
        mine[pl.ds(block * per, per)] = result.astype(jnp.bfloat16).reshape(per, rows, dim)
        for s in range(per):
            slot = block * per + s
            peer = copy * heads + slot

            @pl.when(peer != me)
            def _():
                pltpu.make_async_remote_copy(
                    src_ref=mine.at[slot], dst_ref=back.at[head],
                    send_sem=back_send, recv_sem=back_sem,
                    device_id={"sp": peer}, device_id_type=MESH,
                ).start()

            @pl.when(peer == me)
            def _():
                pltpu.make_async_copy(mine.at[slot], back.at[head], back_sem).start()

    pltpu.make_async_copy(back, back, back_sem).wait()
    for h in range(heads):
        part = slice(h * dim, (h + 1) * dim)
        mixed = gates[0:1, part] * back[h].astype(jnp.float32) + cross[:, part]
        out_ref[0, :, part] = mixed.astype(out_ref.dtype)

    for dst in (k_all, v_all):
        sent = dst.at[pl.ds(0, n - 1)]
        pltpu.make_async_copy(sent, sent, send_sem).wait()
    for side in range(sides):
        for index, dst in enumerate((near_k, near_v)):
            pltpu.make_async_copy(dst.at[side], dst.at[side], cross_send.at[side, index]).wait()
    for buffer, sem in ((q_all, send_sem), (mine, back_send)):

        @pl.when(in_group)
        def _():
            sent = buffer.at[pl.ds(0, heads - 1)]
            pltpu.make_async_copy(sent, sent, sem).wait()

        if copies > 1:

            @pl.when(jnp.logical_not(in_group))
            def _():
                pltpu.make_async_copy(buffer, buffer, sem).wait()


def solution(mesh):
    n, cams = mesh.shape["sp"], mesh.shape["cam"]
    sides = 1 if cams == 2 else 2

    def local(q_self, keys, values, q_cross, timestep, mod_table):
        rows, width = q_self.shape[1], q_self.shape[2]
        dim = width // HEADS
        bf16, f32 = jnp.bfloat16, jnp.float32
        per = 4
        blocks = HEADS // per
        hbm = pl.BlockSpec(memory_space=pl.ANY)
        return pl.pallas_call(
            functools.partial(kernel, n, cams),
            out_shape=jax.ShapeDtypeStruct(q_self.shape, bf16),
            in_specs=[pl.BlockSpec(memory_space=pltpu.SMEM)] + [hbm] * 5,
            out_specs=pl.BlockSpec(memory_space=pltpu.VMEM),
            scratch_shapes=[
                pltpu.VMEM((HEADS, rows, dim), bf16),
                pltpu.VMEM((n, rows, dim), bf16),
                pltpu.VMEM((n, rows, dim), bf16),
                pltpu.VMEM((sides, rows, width), bf16),
                pltpu.VMEM((sides, rows, width), bf16),
                pltpu.VMEM((rows, width), bf16),
                pltpu.VMEM(mod_table.shape, f32),
                pltpu.VMEM((blocks, per * rows, n * rows), bf16),
                pltpu.VMEM((blocks, per * rows, 1), f32),
                pltpu.VMEM((HEADS, rows, dim), bf16),
                pltpu.VMEM((HEADS, rows, dim), bf16),
                pltpu.VMEM((rows, width), f32),
                pltpu.SemaphoreType.DMA,
                pltpu.SemaphoreType.DMA((sides, 2)),
                pltpu.SemaphoreType.DMA,
                pltpu.SemaphoreType.DMA,
                pltpu.SemaphoreType.DMA,
                pltpu.SemaphoreType.DMA,
                pltpu.SemaphoreType.DMA((sides, 2)),
                pltpu.SemaphoreType.DMA,
                pltpu.SemaphoreType.DMA,
                pltpu.SemaphoreType.DMA,
            ],
            compiler_params=pltpu.CompilerParams(
                collective_id=0, has_side_effects=True, vmem_limit_bytes=60 * 1024 * 1024
            ),
        )(timestep, q_self, keys, values, q_cross, mod_table)

    placed = P("cam", "sp", None)
    return jax.shard_map(
        local,
        mesh=mesh,
        in_specs=(placed, placed, placed, placed, P(), P()),
        out_specs=placed,
        check_vma=False,
    )
```

```python
import functools
import math

import jax
import jax.numpy as jnp
from jax import lax
from jax.experimental import pallas as pl
from jax.experimental.pallas import tpu as pltpu
from jax.sharding import PartitionSpec as P

HEADS = 16
GROUPS = 4
MESH = pl.DeviceIdType.MESH
LOG2E = 1.4426950408889634


def offsets(count):
    return sorted(range(1, count), key=lambda d: (-abs(d - count // 2), d))


def softmax_parts(scores, scale):
    peak = jnp.max(scores, axis=-1, keepdims=True)
    weights = jnp.exp2((scores - peak) * (scale * LOG2E))
    return weights.astype(jnp.bfloat16), jnp.sum(weights, axis=-1, keepdims=True)


def dot_t(a, b):
    return lax.dot_general(a, b, (((1,), (1,)), ((), ())), preferred_element_type=jnp.float32)


def kernel(
    n, cams, step_in, q_ref, k_ref, v_ref, qc_ref, mod_ref, out_ref,
    q_all, k_all, v_all, near_k, near_v, qc, mod, step_ref, mine, back, cross,
    send_sem, cross_send, back_send, q_sem, k_sem, v_sem, near_sem, back_sem, qc_sem, mod_sem, step_sem,
):
    rows, dim = q_all.shape[1], q_all.shape[2]
    heads = HEADS
    copies = n // heads
    sides = near_k.shape[0]
    me = lax.axis_index("sp")
    cam = lax.axis_index("cam")
    head = lax.div(me, copies)
    copy = lax.rem(me, copies)
    my_group = lax.div(me, heads)
    my_slot = lax.rem(me, heads)
    scale = 1.0 / math.sqrt(dim)
    order = offsets(heads) + [0]
    groups = q_sem.shape[0]
    per = heads // groups

    def cols(h):
        return pl.ds(pl.multiple_of(h * dim, dim), dim)

    barrier = pltpu.get_barrier_semaphore()
    for d in offsets(n):
        pl.semaphore_signal(
            barrier, inc=1, device_id={"sp": lax.rem(me + d, n)}, device_id_type=MESH
        )
    for side in range(sides):
        other = lax.rem(cam + (1 if side == 0 else cams - 1), cams)
        pl.semaphore_signal(barrier, inc=1, device_id={"cam": other}, device_id_type=MESH)

    load_qc = pltpu.make_async_copy(qc_ref.at[0], qc, qc_sem)
    load_mod = pltpu.make_async_copy(mod_ref, mod, mod_sem)
    load_qc.start()
    load_mod.start()
    load_step = pltpu.make_async_copy(step_in, step_ref, step_sem)
    load_step.start()
    pltpu.make_async_copy(k_ref.at[0, :, cols(head)], k_all.at[me], k_sem).start()
    pltpu.make_async_copy(v_ref.at[0, :, cols(head)], v_all.at[me], v_sem).start()
    pl.semaphore_wait(barrier, n - 1 + sides)

    def send(src, dst, sem, peer):
        pltpu.make_async_remote_copy(
            src_ref=src, dst_ref=dst, send_sem=send_sem, recv_sem=sem,
            device_id={"sp": peer}, device_id_type=MESH,
        ).start()

    for src, dst, sem in ((k_ref, k_all, k_sem), (v_ref, v_all, v_sem)):
        for d in offsets(n):
            peer = lax.rem(me + d, n)
            send(src.at[0, :, cols(lax.div(peer, copies))], dst.at[me], sem, peer)

    def by_place(d, peer, far, near):
        if copies == 1:
            (far if d else near)()
        else:
            pl.when(peer != me)(far)
            pl.when(peer == me)(near)

    for i, d in enumerate(order):
        target = lax.rem(my_slot + d, heads)
        peer = target * copies + my_group
        src, dst, sem = q_ref.at[0, :, cols(target)], q_all.at[i], q_sem.at[i // per]
        by_place(
            d, peer,
            lambda: send(src, dst, sem, peer),
            lambda: pltpu.make_async_copy(src, dst, sem).start(),
        )

    for side in range(sides):
        other = lax.rem(cam + (1 if side == 0 else cams - 1), cams)
        for index, (src, dst) in enumerate(((k_ref, near_k), (v_ref, near_v))):
            pltpu.make_async_remote_copy(
                src_ref=src.at[0], dst_ref=dst.at[side],
                send_sem=cross_send.at[side, index], recv_sem=near_sem.at[side, index],
                device_id={"cam": other}, device_id_type=MESH,
            ).start()
    pltpu.make_async_copy(k_all, k_all, k_sem).wait()
    pltpu.make_async_copy(v_all, v_all, v_sem).wait()
    keys = k_all[...].reshape(n * rows, dim)
    vals = v_all[...].reshape(n * rows, dim)
    for g in range(groups):
        here = pl.ds(g * per, per)
        pltpu.make_async_copy(q_all.at[here], q_all.at[here], q_sem.at[g]).wait()
        w, total = softmax_parts(dot_t(q_all[here].reshape(per * rows, dim), keys), scale)
        result = jnp.dot(w, vals, preferred_element_type=jnp.float32) / total
        mine[here] = result.astype(jnp.bfloat16).reshape(per, rows, dim)
        for i in range(g * per, (g + 1) * per):
            d = order[i]
            peer = copy * heads + lax.rem(head + heads - d, heads)
            src, dst = mine.at[i], back.at[head]
            by_place(
                d, peer,
                lambda: pltpu.make_async_remote_copy(
                    src_ref=src, dst_ref=dst, send_sem=back_send, recv_sem=back_sem,
                    device_id={"sp": peer}, device_id_type=MESH,
                ).start(),
                lambda: pltpu.make_async_copy(src, dst, back_sem).start(),
            )

    load_qc.wait()
    load_mod.wait()
    load_step.wait()
    for side in range(sides):
        for index, dst in enumerate((near_k, near_v)):
            pltpu.make_async_copy(dst.at[side], dst.at[side], near_sem.at[side, index]).wait()
    gates = mod[step_ref[0]]
    for h in range(heads):
        part = slice(h * dim, (h + 1) * dim)
        keys = near_k[:, :, part].reshape(sides * rows, dim)
        vals = near_v[:, :, part].reshape(sides * rows, dim)
        w, total = softmax_parts(dot_t(qc[:, part], keys), scale)
        result = jnp.dot(w, vals, preferred_element_type=jnp.float32) / total
        cross[:, part] = gates[1:2, part] * result

    pltpu.make_async_copy(back, back, back_sem).wait()
    for h in range(heads):
        part = slice(h * dim, (h + 1) * dim)
        mixed = gates[0:1, part] * back[h].astype(jnp.float32) + cross[:, part]
        out_ref[0, :, part] = mixed.astype(out_ref.dtype)

    for dst in (k_all, v_all):
        sent = dst.at[pl.ds(0, n - 1)]
        pltpu.make_async_copy(sent, sent, send_sem).wait()
    for side in range(sides):
        for index, dst in enumerate((near_k, near_v)):
            pltpu.make_async_copy(dst.at[side], dst.at[side], cross_send.at[side, index]).wait()
    for buffer, sem in ((q_all, send_sem), (mine, back_send)):
        sent = buffer.at[pl.ds(0, heads - 1)]
        rest = buffer.at[0]
        pltpu.make_async_copy(sent, sent, sem).wait()
        if copies > 1:

            @pl.when(my_group != copy)
            def _():
                pltpu.make_async_copy(rest, rest, sem).wait()


def solution(mesh):
    n, cams = mesh.shape["sp"], mesh.shape["cam"]
    sides = 1 if cams == 2 else 2

    def local(q_self, keys, values, q_cross, timestep, mod_table):
        rows, width = q_self.shape[1], q_self.shape[2]
        dim = width // HEADS
        bf16, f32 = jnp.bfloat16, jnp.float32
        hbm = pl.BlockSpec(memory_space=pl.ANY)
        return pl.pallas_call(
            functools.partial(kernel, n, cams),
            out_shape=pltpu.VMEM(q_self.shape, bf16),
            in_specs=[hbm] * 6,
            out_specs=pl.BlockSpec(memory_space=pltpu.VMEM),
            scratch_shapes=[
                pltpu.VMEM((HEADS, rows, dim), bf16),
                pltpu.VMEM((n, rows, dim), bf16),
                pltpu.VMEM((n, rows, dim), bf16),
                pltpu.VMEM((sides, rows, width), bf16),
                pltpu.VMEM((sides, rows, width), bf16),
                pltpu.VMEM((rows, width), bf16),
                pltpu.VMEM(mod_table.shape, f32),
                pltpu.SMEM(timestep.shape, jnp.int32),
                pltpu.VMEM((HEADS, rows, dim), bf16),
                pltpu.VMEM((HEADS, rows, dim), bf16),
                pltpu.VMEM((rows, width), f32),
                pltpu.SemaphoreType.DMA,
                pltpu.SemaphoreType.DMA((sides, 2)),
                pltpu.SemaphoreType.DMA,
                pltpu.SemaphoreType.DMA((GROUPS,)),
                pltpu.SemaphoreType.DMA,
                pltpu.SemaphoreType.DMA,
                pltpu.SemaphoreType.DMA((sides, 2)),
                pltpu.SemaphoreType.DMA,
                pltpu.SemaphoreType.DMA,
                pltpu.SemaphoreType.DMA,
                pltpu.SemaphoreType.DMA,
            ],
            compiler_params=pltpu.CompilerParams(
                collective_id=0, has_side_effects=True, vmem_limit_bytes=60 * 1024 * 1024
            ),
        )(timestep, q_self, keys, values, q_cross, mod_table)

    placed = P("cam", "sp", None)
    return jax.shard_map(
        local,
        mesh=mesh,
        in_specs=(placed, placed, placed, placed, P(), P()),
        out_specs=placed,
        check_vma=False,
    )
```

```python
import functools
import math

import jax
import jax.numpy as jnp
from jax import lax
from jax.experimental import pallas as pl
from jax.experimental.pallas import tpu as pltpu
from jax.sharding import PartitionSpec as P

HEADS = 16
GROUPS = 4
MESH = pl.DeviceIdType.MESH
LOG2E = 1.4426950408889634


def flipped(place, count):
    bits = [1 << b for b in range(count.bit_length() - 1)]
    moves = [bit * (1 - 2 * lax.rem(lax.div(place, bit), 2)) for bit in bits]

    def at(d):
        return place + sum(move for bit, move in zip(bits, moves) if d & bit)

    return at


def softmax_parts(scores, scale):
    peak = jnp.max(scores, axis=-1, keepdims=True)
    weights = jnp.exp2((scores - peak) * (scale * LOG2E))
    return weights.astype(jnp.bfloat16), jnp.sum(weights, axis=-1, keepdims=True)


def dot_t(a, b):
    return lax.dot_general(a, b, (((1,), (1,)), ((), ())), preferred_element_type=jnp.float32)


def kernel(
    n, cams, step_in, q_ref, k_ref, v_ref, qc_ref, mod_ref, out_ref,
    q_all, k_all, v_all, near_k, near_v, qc, mod, step_ref, mine, back, cross,
    send_sem, cross_send, back_send, q_sem, k_sem, v_sem, near_sem, back_sem, qc_sem, mod_sem, step_sem,
):
    rows, dim = q_all.shape[1], q_all.shape[2]
    heads = HEADS
    copies = n // heads
    sides = near_k.shape[0]
    me = lax.axis_index("sp")
    cam = lax.axis_index("cam")
    head = lax.div(me, copies)
    copy = lax.rem(me, copies)
    my_group = lax.div(me, heads)
    my_slot = lax.rem(me, heads)
    scale = 1.0 / math.sqrt(dim)
    peer_at = flipped(me, n)
    target_at = flipped(my_slot, heads)
    source_at = flipped(head, heads)
    order = list(range(heads - 1, -1, -1))
    groups = q_sem.shape[0]
    per = heads // groups

    def cols(h):
        return pl.ds(pl.multiple_of(h * dim, dim), dim)

    barrier = pltpu.get_barrier_semaphore()
    for d in range(1, n):
        pl.semaphore_signal(barrier, inc=1, device_id={"sp": peer_at(d)}, device_id_type=MESH)
    for side in range(sides):
        other = lax.rem(cam + (1 if side == 0 else cams - 1), cams)
        pl.semaphore_signal(barrier, inc=1, device_id={"cam": other}, device_id_type=MESH)

    load_qc = pltpu.make_async_copy(qc_ref.at[0], qc, qc_sem)
    load_mod = pltpu.make_async_copy(mod_ref, mod, mod_sem)
    load_qc.start()
    load_mod.start()
    load_step = pltpu.make_async_copy(step_in, step_ref, step_sem)
    load_step.start()
    pltpu.make_async_copy(k_ref.at[0, :, cols(head)], k_all.at[me], k_sem).start()
    pltpu.make_async_copy(v_ref.at[0, :, cols(head)], v_all.at[me], v_sem).start()
    pl.semaphore_wait(barrier, n - 1 + sides)

    def send(src, dst, sem, peer):
        pltpu.make_async_remote_copy(
            src_ref=src, dst_ref=dst, send_sem=send_sem, recv_sem=sem,
            device_id={"sp": peer}, device_id_type=MESH,
        ).start()

    for d in range(1, n):
        peer = peer_at(d)
        for src, dst, sem in ((k_ref, k_all, k_sem), (v_ref, v_all, v_sem)):
            send(src.at[0, :, cols(lax.div(peer, copies))], dst.at[me], sem, peer)

    def by_place(d, peer, far, near):
        if copies == 1:
            (far if d else near)()
        else:
            pl.when(peer != me)(far)
            pl.when(peer == me)(near)

    for i, d in enumerate(order):
        target = target_at(d)
        peer = target * copies + my_group
        src, dst, sem = q_ref.at[0, :, cols(target)], q_all.at[i], q_sem.at[i // per]
        by_place(
            d, peer,
            lambda: send(src, dst, sem, peer),
            lambda: pltpu.make_async_copy(src, dst, sem).start(),
        )

    for side in range(sides):
        other = lax.rem(cam + (1 if side == 0 else cams - 1), cams)
        for index, (src, dst) in enumerate(((k_ref, near_k), (v_ref, near_v))):
            pltpu.make_async_remote_copy(
                src_ref=src.at[0], dst_ref=dst.at[side],
                send_sem=cross_send.at[side, index], recv_sem=near_sem.at[side, index],
                device_id={"cam": other}, device_id_type=MESH,
            ).start()
    pltpu.make_async_copy(k_all, k_all, k_sem).wait()
    pltpu.make_async_copy(v_all, v_all, v_sem).wait()
    keys = k_all[...].reshape(n * rows, dim)
    vals = v_all[...].reshape(n * rows, dim)
    for g in range(groups):
        here = pl.ds(g * per, per)
        pltpu.make_async_copy(q_all.at[here], q_all.at[here], q_sem.at[g]).wait()
        w, total = softmax_parts(dot_t(q_all[here].reshape(per * rows, dim), keys), scale)
        result = jnp.dot(w, vals, preferred_element_type=jnp.float32) / total
        mine[here] = result.astype(jnp.bfloat16).reshape(per, rows, dim)
        for i in range(g * per, (g + 1) * per):
            d = order[i]
            peer = copy * heads + source_at(d)
            src, dst = mine.at[i], back.at[i]
            sem = back_sem.at[g]
            by_place(
                d, peer,
                lambda: pltpu.make_async_remote_copy(
                    src_ref=src, dst_ref=dst, send_sem=back_send, recv_sem=sem,
                    device_id={"sp": peer}, device_id_type=MESH,
                ).start(),
                lambda: pltpu.make_async_copy(src, dst, sem).start(),
            )

    load_qc.wait()
    load_mod.wait()
    load_step.wait()
    for side in range(sides):
        for index, dst in enumerate((near_k, near_v)):
            pltpu.make_async_copy(dst.at[side], dst.at[side], near_sem.at[side, index]).wait()
    gates = mod[step_ref[0]]
    for h in range(heads):
        part = slice(h * dim, (h + 1) * dim)
        keys = near_k[:, :, part].reshape(sides * rows, dim)
        vals = near_v[:, :, part].reshape(sides * rows, dim)
        w, total = softmax_parts(dot_t(qc[:, part], keys), scale)
        result = jnp.dot(w, vals, preferred_element_type=jnp.float32) / total
        cross[:, part] = gates[1:2, part] * result

    for g in range(groups):
        here = pl.ds(g * per, per)
        pltpu.make_async_copy(back.at[here], back.at[here], back_sem.at[g]).wait()
        for i in range(g * per, (g + 1) * per):
            part = cols(target_at(order[i]))
            gate = mod[step_ref[0], :, part][0:1]
            mixed = gate * back[i].astype(jnp.float32) + cross[:, part]
            out_ref[0, :, part] = mixed.astype(out_ref.dtype)

    for dst in (k_all, v_all):
        sent = dst.at[pl.ds(0, n - 1)]
        pltpu.make_async_copy(sent, sent, send_sem).wait()
    for side in range(sides):
        for index, dst in enumerate((near_k, near_v)):
            pltpu.make_async_copy(dst.at[side], dst.at[side], cross_send.at[side, index]).wait()
    for buffer, sem in ((q_all, send_sem), (mine, back_send)):
        sent = buffer.at[pl.ds(0, heads - 1)]
        rest = buffer.at[0]
        pltpu.make_async_copy(sent, sent, sem).wait()
        if copies > 1:

            @pl.when(my_group != copy)
            def _():
                pltpu.make_async_copy(rest, rest, sem).wait()


def solution(mesh):
    n, cams = mesh.shape["sp"], mesh.shape["cam"]
    sides = 1 if cams == 2 else 2

    def local(q_self, keys, values, q_cross, timestep, mod_table):
        rows, width = q_self.shape[1], q_self.shape[2]
        dim = width // HEADS
        bf16, f32 = jnp.bfloat16, jnp.float32
        hbm = pl.BlockSpec(memory_space=pl.ANY)
        return pl.pallas_call(
            functools.partial(kernel, n, cams),
            out_shape=pltpu.VMEM(q_self.shape, bf16),
            in_specs=[hbm] * 6,
            out_specs=pl.BlockSpec(memory_space=pltpu.VMEM),
            scratch_shapes=[
                pltpu.VMEM((HEADS, rows, dim), bf16),
                pltpu.VMEM((n, rows, dim), bf16),
                pltpu.VMEM((n, rows, dim), bf16),
                pltpu.VMEM((sides, rows, width), bf16),
                pltpu.VMEM((sides, rows, width), bf16),
                pltpu.VMEM((rows, width), bf16),
                pltpu.VMEM(mod_table.shape, f32),
                pltpu.SMEM(timestep.shape, jnp.int32),
                pltpu.VMEM((HEADS, rows, dim), bf16),
                pltpu.VMEM((HEADS, rows, dim), bf16),
                pltpu.VMEM((rows, width), f32),
                pltpu.SemaphoreType.DMA,
                pltpu.SemaphoreType.DMA((sides, 2)),
                pltpu.SemaphoreType.DMA,
                pltpu.SemaphoreType.DMA((GROUPS,)),
                pltpu.SemaphoreType.DMA,
                pltpu.SemaphoreType.DMA,
                pltpu.SemaphoreType.DMA((sides, 2)),
                pltpu.SemaphoreType.DMA((GROUPS,)),
                pltpu.SemaphoreType.DMA,
                pltpu.SemaphoreType.DMA,
                pltpu.SemaphoreType.DMA,
            ],
            compiler_params=pltpu.CompilerParams(
                collective_id=0, has_side_effects=True, vmem_limit_bytes=60 * 1024 * 1024
            ),
        )(timestep, q_self, keys, values, q_cross, mod_table)

    placed = P("cam", "sp", None)
    return jax.shard_map(
        local,
        mesh=mesh,
        in_specs=(placed, placed, placed, placed, P(), P()),
        out_specs=placed,
        check_vma=False,
    )
```
